512 devices in a mesh: dp: 16 (over z), owner: 32 (over x, y, core).
Axes of the slice: x: 4, y: 4, z: 16, core: 2. Of those that a mesh axis runs over, the one named last changes fastest.
Arguments:
- grad_partials: bfloat16 [16, 32, 1048576], P('dp', None, 'owner'), may hold values from -2.5 to 2.5
- block_owner: int32 [32], replicated, may hold values from 0 to 31, as said below
- block_slot: int32 [32], replicated, may hold values from 0 to 1
- left_stat: float32 [64, 1024, 1024], P('owner', 'dp'), may hold values from -6 to 6
- right_stat: float32 [64, 1024, 1024], P('owner', 'dp'), may hold values from -6 to 6
- left_root: bfloat16 [64, 1024, 1024], P('owner', 'dp'), may hold values from -0.1875 to 0.1875
- right_root: bfloat16 [64, 1024, 1024], P('owner', 'dp'), may hold values from -0.1875 to 0.1875
Outputs:
- precond: bfloat16 [32, 1048576], P(None, ('dp', 'owner'))
- left_new: float32 [64, 1024, 1024], P('owner', 'dp')
- right_new: float32 [64, 1024, 1024], P('owner', 'dp')
The draws below stay inside these ranges and needn't reach their ends.
Inputs may be any that keep to these rules, and one draw needn't show every extreme that they name: `block_owner`: blocks take distinct pairs of owner and slot; no owner holds more than 2 blocks, and some owner holds exactly 2.
All inputs are finite; a program needn't handle non-finite values.
Results may differ from the reference program's by a relative error of at most 0.025.
Values may be sent and summed in bfloat16 or wider, within the bound.
A program may use at most 64 MiB of HBM per device.

```python
import jax
import jax.numpy as jnp
from jax import lax

BS = 1024
NB = 32
CAP = 2
SLOTS = 64
REPLICAS = 16
N_OWNER = 32


def assignment(key):
    busiest = jax.random.randint(jax.random.fold_in(key, 101), (), 0, N_OWNER)
    places = jnp.arange(SLOTS, dtype=jnp.int32)
    scores = jax.random.permutation(jax.random.fold_in(key, 102), SLOTS).astype(jnp.int32)
    scores = jnp.where(places // CAP == busiest, -1 - places % CAP, scores)
    scores = jnp.where(places == 0, -CAP - 1, scores)
    scores = jnp.where(places == (N_OWNER - 1) * CAP, -CAP - 2, scores)
    ranked = jnp.argsort(scores, stable=True).astype(jnp.int32)[:NB]
    shuffle = jax.random.permutation(jax.random.fold_in(key, 103), NB).astype(jnp.int32)
    chosen = ranked[shuffle]
    return ((chosen // CAP).astype(jnp.int32), (chosen % CAP).astype(jnp.int32))


def draw_block_owner(key, part):
    return assignment(key)[0]


def draw_block_slot(key, part):
    return assignment(key)[1]


def strengthened(values, stream_key, source, target, parts, factor):
    def block_of(dim):
        return (jnp.arange(values.shape[dim]) // (values.shape[dim] // parts)).reshape((-1,) + (1,) * (values.ndim - 1 - dim))

    first = jax.random.permutation(stream_key, parts)[block_of(target)]
    far = (block_of(target) + parts // 2) % parts
    return jnp.where((block_of(source) == first) | (block_of(source) == far), factor * values, values)


def block_scale(own_key, dims, split, least, high):
    factor_of = 1.0
    for dim, parts in split:
        draws = jax.random.uniform(jax.random.fold_in(jax.random.fold_in(own_key, 6), dim), (parts,), jnp.float32, least / len(split), high / len(split))
        factor_of = factor_of * jnp.repeat(jnp.exp(draws), dims[dim] // parts).reshape((-1,) + (1,) * (len(dims) - 1 - dim))
    return factor_of


def centred(rng, dims, deviation, bound, pieces=(), held_as=jnp.bfloat16):
    values = jax.random.normal(rng, dims, jnp.float32) * deviation
    if len(pieces) > 0:
        values = block_scale(rng, dims, pieces, -0.22, 0.18) * values
    return jnp.clip(values, min=-bound, max=bound).astype(held_as)


def heavy_noise(own_key, extent, scale, limit, shards, heavy, kind=jnp.bfloat16):
    array = scale * jax.random.normal(own_key, extent, jnp.float32)
    if shards:
        array = array * block_scale(own_key, extent, shards, -0.22, 0.18)
    return jnp.clip(strengthened(array, jax.random.fold_in(own_key, 3), *heavy), -limit, limit).astype(kind)


def setup_inputs(seed: int = 0) -> dict:
    keys = jax.random.split(jax.random.key(seed), 8)
    return {
        "grad_partials": heavy_noise(keys[0], (REPLICAS, NB, BS * BS), 0.125, 2.5, ((0, 16), (2, 32)), (0, 2, 16, 2.0)),
        "block_owner": draw_block_owner(jax.random.fold_in(keys[7], 71), 0),
        "block_slot": draw_block_slot(jax.random.fold_in(keys[7], 71), 0),
        "left_stat": centred(keys[3], (SLOTS, BS, BS), 1.0, 6.0, ((0, 32), (1, 16)), jnp.float32),
        "right_stat": centred(keys[4], (SLOTS, BS, BS), 1.0, 6.0, ((0, 32), (1, 16)), jnp.float32),
        "left_root": centred(keys[5], (SLOTS, BS, BS), BS ** -0.5, 0.1875, ((0, 32), (1, 16))),
        "right_root": centred(keys[6], (SLOTS, BS, BS), BS ** -0.5, 0.1875, ((0, 32), (1, 16))),
    }


decay_rate = 0.95


def reference(grad_partials, block_owner, block_slot, left_stat, right_stat, left_root, right_root):
    gradient = jnp.sum(grad_partials, axis=0, dtype=jnp.float32).astype(jnp.bfloat16)
    slot_ids = (block_owner * CAP + block_slot).astype(jnp.int32)

    def per_block(inputs):
        flat_block, root_left, root_right = inputs
        matrix = flat_block.reshape(BS, BS)
        left_gram = jnp.dot(matrix, matrix.T, preferred_element_type=jnp.float32)
        right_gram = jnp.dot(matrix.T, matrix, preferred_element_type=jnp.float32)
        scaled = jnp.dot(root_left, matrix, preferred_element_type=jnp.float32).astype(jnp.bfloat16)
        result = jnp.dot(scaled, root_right, preferred_element_type=jnp.float32).astype(jnp.bfloat16)
        return left_gram, right_gram, result.reshape(BS * BS)

    left_grams, right_grams, precond = lax.map(per_block, (gradient, left_root[slot_ids], right_root[slot_ids]))
    blank_stats = jnp.zeros(left_stat.shape, jnp.float32)
    left_new = decay_rate * left_stat + (1.0 - decay_rate) * blank_stats.at[slot_ids].set(left_grams)
    right_new = decay_rate * right_stat + (1.0 - decay_rate) * blank_stats.at[slot_ids].set(right_grams)
    return precond, left_new, right_new
```

```python
import functools

import jax
import jax.numpy as jnp
from jax import lax
from jax.experimental import pallas as pl
from jax.experimental.pallas import tpu as pltpu
from jax.sharding import PartitionSpec as P

decay_rate = 0.95

MESH = pl.DeviceIdType.MESH
BF16 = jnp.bfloat16
F32 = jnp.float32
PLANES = 16
OWNERS = 32
BLOCKS = 32
WIDTH = 1024
SUBS = 2


def iotas(rows, columns):
    return (
        lax.broadcasted_iota(jnp.int32, (rows, columns), 0),
        lax.broadcasted_iota(jnp.int32, (rows, columns), 1),
    )


def one_hot(hit):
    return jnp.where(hit, 1.0, 0.0).astype(BF16)


def mix(chooser, data):
    return jnp.dot(chooser, data, preferred_element_type=F32).astype(BF16)


def times_transposed(a, b):
    return lax.dot_general(a, b, (((1,), (1,)), ((), ())), preferred_element_type=F32)


def chunk(start, size, unit=None):
    return pl.ds(pl.multiple_of(start, unit or size), size)


def shuffles():
    m, k = iotas(256, 256)
    transpose16 = (m % 16) * 16 + m // 16
    roots_out = (((m >> 4) & 1) * 32 + ((m >> 3) & 1) * 16 + (m & 3) * 4) * 4 + (m >> 5) * 2 + ((m >> 2) & 1)
    stats_in = ((m >> 1) & 7) * 32 + (m >> 7) * 16 + ((m >> 6) & 1) * 8 + (m & 1) * 4 + ((m >> 4) & 3)
    roots_in = ((m >> 1) & 15) * 16 + (m >> 7) * 8 + (m & 1) * 4 + ((m >> 5) & 3)
    grams_out = ((((m >> 3) & 1) * 4 + (m & 3)) * 16 + (m >> 4)) * 2 + ((m >> 2) & 1)
    scaled_out = ((m & 7) * 16 + (m >> 4)) * 2 + ((m >> 3) & 1)
    right_rows = ((m >> 2) & 3) * 64 + (m >> 4) * 4 + (m & 3)
    return [one_hot(k == s) for s in (transpose16, roots_out, stats_in, roots_in, grams_out, scaled_out, right_rows)]


T16, ROOTS_OUT, STATS_IN, ROOTS_IN, GRAMS_OUT, SCALED_OUT, RIGHT_ROWS = range(7)


class Spread:
    def __init__(self, buf, send_sem, recv_sem, place):
        self.buf, self.send_sem, self.recv_sem = buf, send_sem, recv_sem
        self.z, self.x, self.y, self.c = place

    def chip(self, h, da, db):
        first, second = (self.x, self.y) if h == 0 else (self.y, self.x)
        first, second = (first + da) % 4, (second + db) % 4
        return (first, second) if h == 0 else (second, first)

    def piece(self, h, da, db, half=None):
        px, py = self.chip(h, da, db)
        start = px * 256 + py * 64 + (self.c if h == 0 else 1 - self.c) * 32
        if half is None:
            return self.buf.at[chunk(start, 32)]
        return self.buf.at[chunk(start + 16 * half, 16)]

    def copy(self, h, da, db, half, axis, delta):
        px, py = self.chip(h, delta if axis == 0 else 0, delta if axis == 1 else 0)
        there = ((da - delta) % 4, db) if axis == 0 else (da, (db - delta) % 4)
        ref = self.piece(h, da, db, half)
        return pltpu.make_async_remote_copy(
            src_ref=ref,
            dst_ref=ref,
            send_sem=self.send_sem,
            recv_sem=self.recv_sem.at[h, there[0], there[1], half or 0],
            device_id=(self.z, (px * 4 + py) * 2 + self.c),
            device_id_type=MESH,
        )

    def wait(self, h, da, db, half=None):
        ref = self.piece(h, da, db, half)
        pltpu.make_async_copy(ref, ref, self.recv_sem.at[h, da, db, half or 0]).wait()

    def across(self, h, da):
        for delta in (1, -1):
            self.copy(h, da, 0, None, 1, delta).start()

    def begin(self, h):
        for delta in (1, -1):
            self.copy(h, 0, 0, None, 0, delta).start()
        self.across(h, 0)

    def middle(self):
        for da, half, delta in ((3, 0, 1), (1, 1, -1)):
            for h in (0, 1):
                self.wait(h, da, 0)
                self.copy(h, da, 0, half, 0, delta).start()
                self.across(h, da)
        self.turn(0)
        for h in (0, 1):
            self.wait(h, 2, 0, 0)
            self.wait(h, 2, 0, 1)
            self.across(h, 2)
        self.turn(3)
        self.turn(1)
        self.turn(2)

    def turn(self, da):
        for db, half, delta in ((3, 0, 1), (1, 1, -1)):
            for h in (0, 1):
                self.wait(h, da, db)
                self.copy(h, da, db, half, 1, delta).start()

    def end(self):
        for da in (0, 3, 1, 2):
            for h in (0, 1):
                self.wait(h, da, 2, 0)
                self.wait(h, da, 2, 1)

    def sent(self):
        ref = self.buf.at[pl.ds(0, 960)]
        pltpu.make_async_copy(ref, ref, self.send_sem).wait()


class Column:
    def __init__(self, src, dst, sems, place):
        self.src, self.dst, self.sems = src, dst, sems
        self.z, self.chip, self.c = place

    def copy(self, zd, e):
        return pltpu.make_async_remote_copy(
            src_ref=self.src.at[chunk((2 * zd + e) * 16, 16)],
            dst_ref=self.dst.at[chunk((2 * self.z + self.c) * 16, 16)],
            send_sem=self.sems.at[0],
            recv_sem=self.sems.at[1],
            device_id=(zd, 2 * self.chip + e),
            device_id_type=MESH,
        )

    def start(self):
        def step(j, carry):
            for zd in ((self.z + j) % PLANES, (self.z + PLANES - j) % PLANES):
                for e in (0, 1):
                    self.copy(zd, e).start()
            return carry

        lax.fori_loop(1, PLANES // 2, step, 0)
        for e in (0, 1):
            self.copy((self.z + PLANES // 2) % PLANES, e).start()
        self.copy(self.z, 1 - self.c).start()
        own = chunk((2 * self.z + self.c) * 16, 16)
        self.dst[own, :] = self.src[own, :]

    def wait(self, which):
        ref = self.dst.at[pl.ds(0, 31 * 16)]
        pltpu.make_async_copy(ref, ref, self.sems.at[which]).wait()


class Plane:
    def __init__(self, src, dst, sems, place):
        self.src, self.dst, self.sems = src, dst, sems
        self.z, self.o = place

    def start(self):
        def step(j, carry):
            there = (self.o + j) % OWNERS
            pltpu.make_async_remote_copy(
                src_ref=self.src.at[chunk(there * 32, 32)],
                dst_ref=self.dst.at[chunk(self.o * 32, 32)],
                send_sem=self.sems.at[0],
                recv_sem=self.sems.at[1],
                device_id=(self.z, there),
                device_id_type=MESH,
            ).start()
            return carry

        lax.fori_loop(1, OWNERS, step, 0)
        own = chunk(self.o * 32, 32)
        self.dst[own, :] = self.src[own, :]

    def wait(self, which):
        ref = self.dst.at[pl.ds(0, 31 * 32)]
        pltpu.make_async_copy(ref, ref, self.sems.at[which]).wait()


def kernel(
    owner_ref, slot_ref, g_hbm, lstat_hbm, rstat_hbm, lroot_hbm, rroot_hbm,
    precond_ref, left_ref, right_ref,
    g, lstat, rstat, lroot, rroot, perm, parts, from_left, from_right, swapped, block,
    roots_out, roots_in, blocks_out, blocks_in, lsel, rheld, rfull,
    grams, zout, zin, stats_out, stats_in, pout, pin, to_blocks, to_places,
    load_sem, rs_send, right_sem, left_sem, swap_sem, block_send, block_recv, rheld_send, rheld_recv,
    a1_sem, a2_sem, zg_sem, zp_sem, f_sem,
):
    z, o = lax.axis_index("dp"), lax.axis_index("owner")
    chip, c = o // 2, o % 2
    x, y = chip // 4, chip % 4

    loads = [
        pltpu.make_async_copy(src, dst, load_sem.at[n])
        for n, (src, dst) in enumerate(
            ((g_hbm.at[0], g), (lroot_hbm, lroot), (rroot_hbm, rroot), (lstat_hbm, lstat), (rstat_hbm, rstat))
        )
    ]
    for load in loads:
        load.start()

    barrier = pltpu.get_barrier_semaphore()

    def greet_plane(j, carry):
        pl.semaphore_signal(barrier, inc=1, device_id=(z, (o + j) % OWNERS), device_id_type=MESH)
        return carry

    def greet_column(j, carry):
        for e in (0, 1):
            pl.semaphore_signal(barrier, inc=1, device_id=((z + j) % PLANES, 2 * chip + e), device_id_type=MESH)
        return carry

    lax.fori_loop(1, PLANES, greet_column, 0)
    lax.fori_loop(1, OWNERS, greet_plane, 0)

    for n, shuffle in enumerate(shuffles()):
        perm[n] = shuffle

    loads[0].wait()
    for h in range(2):
        for q in range(2):
            for w in range(4):
                columns = [(16 * q + r) * WIDTH + 256 * w for r in range(16)]
                stacked = jnp.concatenate([g[16 * h : 16 * h + 16, n : n + 256] for n in columns], axis=0)
                turned = mix(perm[T16], stacked)
                for b in range(16):
                    at = (b % 2) * 32 + 16 * q
                    parts[8 * h + b // 2, at : at + 16, 256 * w : 256 * w + 256] = turned[16 * b : 16 * b + 16]

    pl.semaphore_wait(barrier, OWNERS - 1 + 2 * (PLANES - 1))

    step_rows = 64 // SUBS

    def rs_copy(right, s, sub):
        rows = pl.ds(sub * step_rows, step_rows)
        held = from_left if right else from_right
        part = (z + 8 - s) % PLANES if right else (z + 9 + s) % PLANES
        sems = right_sem if right else left_sem
        return pltpu.make_async_remote_copy(
            src_ref=parts.at[part, rows] if s == 0 else held.at[s - 1, rows],
            dst_ref=held.at[s, rows],
            send_sem=rs_send,
            recv_sem=sems.at[s, sub],
            device_id=((z + (1 if right else PLANES - 1)) % PLANES, o),
            device_id_type=MESH,
        )

    def rs_step(right, s, sub):
        if s > 0:
            rs_copy(right, s - 1, sub).wait_recv()
            rows = pl.ds(sub * step_rows, step_rows)
            held = from_left if right else from_right
            part = (z + 8 - s) % PLANES if right else (z + 9 + s) % PLANES
            total = held[s - 1, rows, :].astype(F32) + parts[part, rows, :].astype(F32)
            held[s - 1, rows, :] = total.astype(BF16)
        rs_copy(right, s, sub).start()

    for sub in range(SUBS):
        rs_step(True, 0, sub)
        rs_step(False, 0, sub)

    loads[1].wait()
    loads[2].wait()
    for k in range(4):
        stacked = jnp.concatenate(
            [
                root[p, 16 * k : 16 * k + 16, 256 * q : 256 * q + 256]
                for p in range(2)
                for root in (lroot, rroot)
                for q in range(4)
            ],
            axis=0,
        )
        roots_out[256 * k : 256 * k + 256, :] = mix(perm[ROOTS_OUT], stacked)
    a1 = Plane(roots_out, roots_in, a1_sem, (z, o))
    a1.start()

    for sub in range(SUBS):
        rs_step(True, 1, sub)
        rs_step(False, 1, sub)

    places = [owner_ref[b] * 2 + slot_ref[b] for b in range(BLOCKS)]
    row, column = iotas(16, WIDTH)
    for b in range(BLOCKS):
        to_blocks[16 * b : 16 * b + 16, :] = one_hot(column == places[b] * 16 + row)
    column = lax.broadcasted_iota(jnp.int32, (1, 512), 1)
    target = jnp.zeros((1, 512), jnp.int32)
    for b in range(BLOCKS):
        target = jnp.where(column // 16 == b, places[b] * 16, target)
    target = target + column % 16
    for k in range(4):
        row = lax.broadcasted_iota(jnp.int32, (256, 512), 0) + 256 * k
        to_places[256 * k : 256 * k + 256, :] = one_hot(row == target)

    for s in (2, 3):
        for sub in range(SUBS):
            rs_step(True, s, sub)
            rs_step(False, s, sub)

    a1.wait(1)
    blocks_out[...] = mix(to_blocks[...], roots_in[...])

    for s in (4, 5, 6):
        for sub in range(SUBS):
            rs_step(True, s, sub)
            rs_step(False, s, sub)
    for sub in range(SUBS):
        rs_step(True, 7, sub)

    a2 = Column(blocks_out, blocks_in, a2_sem, (z, chip, c))
    a2.start()

    def last_sum(which):
        rows = chunk(which * 32, 32)
        for held, sems, s in ((from_left, right_sem, 7), (from_right, left_sem, 6)):
            if SUBS == 2:
                ref = held.at[s, rows]
                pltpu.make_async_copy(ref, ref, sems.at[s, which]).wait()
            else:
                for n in range(SUBS // 2):
                    ref = held.at[s, chunk(which * 32 + n * step_rows, step_rows)]
                    pltpu.make_async_copy(ref, ref, sems.at[s, which * (SUBS // 2) + n]).wait()
        total = parts[z, rows, :].astype(F32) + from_left[7, rows, :].astype(F32) + from_right[6, rows, :].astype(F32)
        return total.astype(BF16)

    def swap_copy(rows_of):
        return pltpu.make_async_remote_copy(
            src_ref=swapped,
            dst_ref=block.at[chunk(rows_of * 32, 32)],
            send_sem=swap_sem.at[0],
            recv_sem=swap_sem.at[1],
            device_id=(z, 2 * chip + 1 - c),
            device_id_type=MESH,
        )

    swapped[...] = last_sum(1 - c)
    swap_copy(o).start()
    block[chunk(o * 32, 32), :] = last_sum(c)
    spread = Spread(block, block_send, block_recv, (z, x, y, c))
    spread.begin(0)
    swap_copy(2 * chip + 1 - c).wait_recv()
    spread.begin(1)
    spread.middle()

    a2.wait(1)
    for h in range(2):
        turned = mix(perm[ROOTS_IN], blocks_in[256 * h : 256 * h + 256, :])
        for q in range(4):
            lsel[32 * h : 32 * h + 32, 256 * q : 256 * q + 256] = turned[32 * q : 32 * q + 32]
            rheld[chunk(chip * 64 + 32 * h, 32), 256 * q : 256 * q + 256] = turned[128 + 32 * q : 160 + 32 * q]
    rspread = Spread(rheld, rheld_send, rheld_recv, (z, x, y, c))
    rspread.begin(0)
    rspread.begin(1)

    spread.end()

    m, k = iotas(64, 256)
    chosen = one_hot(k == (m >> 2) * 16 + 4 * y + (m & 3))
    stacked = jnp.concatenate([block[chunk(64 * zz + 16 * x, 16), :] for zz in range(PLANES)], axis=0)
    lhs = mix(chosen, stacked)
    for q in range(4):
        grams[0, :, 256 * q : 256 * q + 256] = times_transposed(lhs, block[256 * q : 256 * q + 256, :]).astype(BF16)
    m, k = iotas(64, WIDTH)
    chosen = one_hot(k == (m >> 2) * 64 + 4 * chip + (m & 3))
    lhs = jnp.concatenate(
        [times_transposed(chosen, block[256 * q : 256 * q + 256, :]).astype(BF16) for q in range(4)], axis=1
    )
    for q in range(4):
        grams[1, :, 256 * q : 256 * q + 256] = mix(lhs, block[:, 256 * q : 256 * q + 256])
    for h in range(2):
        stacked = jnp.concatenate(
            [grams[t, 32 * h : 32 * h + 32, 256 * q : 256 * q + 256] for t in range(2) for q in range(4)], axis=0
        )
        zout[256 * h : 256 * h + 256, :] = mix(perm[GRAMS_OUT], stacked)
    zg = Column(zout, zin, zg_sem, (z, chip, c))
    zg.start()

    rspread.middle()
    scaled = jnp.concatenate([mix(lsel[...], block[:, 256 * q : 256 * q + 256]) for q in range(4)], axis=1)
    rspread.end()
    for n in range(4):
        turned = mix(perm[RIGHT_ROWS], rheld[256 * n : 256 * n + 256, :])
        for zz in range(PLANES):
            rfull[64 * zz + 16 * n : 64 * zz + 16 * n + 16, :] = turned[16 * zz : 16 * zz + 16]
    for q in range(4):
        grams[0, :, 256 * q : 256 * q + 256] = mix(scaled, rfull[:, 256 * q : 256 * q + 256])
    for h in range(2):
        stacked = jnp.concatenate(
            [grams[0, 32 * h : 32 * h + 32, 128 * n : 128 * n + 128] for n in range(8)], axis=0
        )
        pout[256 * h : 256 * h + 256, :] = mix(perm[SCALED_OUT], stacked)
    zp = Column(pout, pin, zp_sem, (z, chip, c))
    zp.start()

    zg.wait(1)
    stats_out[...] = mix(to_places[...], zin[...])
    f = Plane(stats_out, stats_in, f_sem, (z, o))
    f.start()

    zp.wait(1)
    for h in range(2):
        turned = mix(perm[T16], pin[256 * h : 256 * h + 256, :])
        for n in range(16):
            precond_ref[16 * h : 16 * h + 16, 128 * n : 128 * n + 128] = turned[16 * n : 16 * n + 16]

    loads[3].wait()
    loads[4].wait()
    f.wait(1)
    for k in range(4):
        turned = jnp.dot(perm[STATS_IN], stats_in[256 * k : 256 * k + 256, :], preferred_element_type=F32)
        for p in range(2):
            for t, (old, new) in enumerate(((lstat, left_ref), (rstat, right_ref))):
                for q in range(4):
                    at = ((p * 2 + t) * 4 + q) * 16
                    there = (p, slice(16 * k, 16 * k + 16), slice(256 * q, 256 * q + 256))
                    new[there] = decay_rate * old[there] + (1.0 - decay_rate) * turned[at : at + 16]

    for held, steps in ((from_left, 8), (from_right, 7)):
        ref = held.at[pl.ds(0, steps)]
        pltpu.make_async_copy(ref, ref, rs_send).wait()
    swap_copy(o).wait_send()
    spread.sent()
    rspread.sent()
    for exchange in (a1, a2, zg, zp, f):
        exchange.wait(0)


def step(grad_partials, block_owner, block_slot, left_stat, right_stat, left_root, right_root):
    vmem = pl.BlockSpec(memory_space=pltpu.VMEM)
    smem = pl.BlockSpec(memory_space=pltpu.SMEM)
    hbm = pl.BlockSpec(memory_space=pl.ANY)
    dma = pltpu.SemaphoreType.DMA
    return pl.pallas_call(
        kernel,
        out_shape=(
            jax.ShapeDtypeStruct((BLOCKS, 2 * WIDTH), BF16),
            jax.ShapeDtypeStruct(left_stat.shape, F32),
            jax.ShapeDtypeStruct(right_stat.shape, F32),
        ),
        in_specs=[smem, smem] + [hbm] * 5,
        out_specs=[vmem] * 3,
        scratch_shapes=[
            pltpu.VMEM((32, 32 * WIDTH), BF16),
            pltpu.VMEM((2, 64, WIDTH), F32),
            pltpu.VMEM((2, 64, WIDTH), F32),
            pltpu.VMEM((2, 64, WIDTH), BF16),
            pltpu.VMEM((2, 64, WIDTH), BF16),
            pltpu.VMEM((7, 256, 256), BF16),
            pltpu.VMEM((16, 64, WIDTH), BF16),
            pltpu.VMEM((8, 64, WIDTH), BF16),
            pltpu.VMEM((7, 64, WIDTH), BF16),
            pltpu.VMEM((32, WIDTH), BF16),
            pltpu.VMEM((WIDTH, WIDTH), BF16),
            pltpu.VMEM((1024, 256), BF16),
            pltpu.VMEM((1024, 256), BF16),
            pltpu.VMEM((512, 256), BF16),
            pltpu.VMEM((512, 256), BF16),
            pltpu.VMEM((64, WIDTH), BF16),
            pltpu.VMEM((WIDTH, WIDTH), BF16),
            pltpu.VMEM((WIDTH, WIDTH), BF16),
            pltpu.VMEM((2, 64, WIDTH), BF16),
            pltpu.VMEM((512, 256), BF16),
            pltpu.VMEM((512, 256), BF16),
            pltpu.VMEM((1024, 256), BF16),
            pltpu.VMEM((1024, 256), BF16),
            pltpu.VMEM((512, 128), BF16),
            pltpu.VMEM((512, 128), BF16),
            pltpu.VMEM((512, 1024), BF16),
            pltpu.VMEM((1024, 512), BF16),
            dma((5,)),
            dma,
            dma((8, SUBS)),
            dma((7, SUBS)),
            dma((2,)),
            dma,
            dma((2, 4, 4, 2)),
            dma,
            dma((2, 4, 4, 2)),
            dma((2,)),
            dma((2,)),
            dma((2,)),
            dma((2,)),
            dma((2,)),
        ],
        compiler_params=pltpu.CompilerParams(
            collective_id=0, has_side_effects=True, vmem_limit_bytes=44 * 1024 * 1024
        ),
    )(block_owner, block_slot, grad_partials, left_stat, right_stat, left_root, right_root)


def solution(mesh):
    return jax.shard_map(
        step,
        mesh=mesh,
        in_specs=(
            P("dp", None, "owner"),
            P(),
            P(),
            P("owner", "dp", None),
            P("owner", "dp", None),
            P("owner", "dp", None),
            P("owner", "dp", None),
        ),
        out_specs=(P(None, ("dp", "owner")), P("owner", "dp", None), P("owner", "dp", None)),
        check_vma=False,
    )
```

```python
import functools

import jax
import jax.numpy as jnp
from jax import lax
from jax.experimental import pallas as pl
from jax.experimental.pallas import tpu as pltpu
from jax.sharding import PartitionSpec as P

decay_rate = 0.95

MESH = pl.DeviceIdType.MESH
BF16 = jnp.bfloat16
F32 = jnp.float32
PLANES = 16
OWNERS = 32
BLOCKS = 32
WIDTH = 1024
SUBS = 4


def iotas(rows, columns):
    return (
        lax.broadcasted_iota(jnp.int32, (rows, columns), 0),
        lax.broadcasted_iota(jnp.int32, (rows, columns), 1),
    )


def one_hot(hit):
    return jnp.where(hit, 1.0, 0.0).astype(BF16)


def mix(chooser, data):
    return jnp.dot(chooser, data, preferred_element_type=F32).astype(BF16)


def times_transposed(a, b):
    return lax.dot_general(a, b, (((1,), (1,)), ((), ())), preferred_element_type=F32)


def chunk(start, size, unit=None):
    return pl.ds(pl.multiple_of(start, unit or size), size)


def transpose16(m):
    return (m % 16) * 16 + m // 16


def roots_out(m):
    return (((m >> 4) & 1) * 32 + ((m >> 3) & 1) * 16 + (m & 3) * 4) * 4 + (m >> 5) * 2 + ((m >> 2) & 1)


def roots_in(m):
    return ((m >> 1) & 15) * 16 + (m >> 7) * 8 + (m & 1) * 4 + ((m >> 5) & 3)


def results_out(m):
    return ((m & 7) * 16 + (m >> 4)) * 2 + ((m >> 3) & 1)


def right_rows(m):
    return ((m >> 2) & 3) * 64 + (m >> 4) * 4 + (m & 3)


def stats_in(m):
    return ((m >> 1) & 7) * 32 + (m >> 7) * 16 + (m & 1) * 8 + ((m >> 4) & 7)


def shuffle(source):
    m, k = iotas(256, 256)
    return one_hot(k == source(m))


SHUFFLES = (transpose16, roots_out, roots_in, results_out, right_rows)
T16, ROOTS_OUT, ROOTS_IN, RESULTS_OUT, RIGHT_ROWS = range(5)


class Spread:
    def __init__(self, buf, send_sem, recv_sem, place):
        self.buf, self.send_sem, self.recv_sem = buf, send_sem, recv_sem
        self.z, self.x, self.y, self.c = place

    def chip(self, h, da, db):
        first, second = (self.x, self.y) if h == 0 else (self.y, self.x)
        first, second = (first + da) % 4, (second + db) % 4
        return (first, second) if h == 0 else (second, first)

    def piece(self, h, da, db, half=None):
        px, py = self.chip(h, da, db)
        start = px * 256 + py * 64 + (self.c if h == 0 else 1 - self.c) * 32
        if half is None:
            return self.buf.at[chunk(start, 32)]
        return self.buf.at[chunk(start + 16 * half, 16)]

    def copy(self, h, da, db, half, axis, delta):
        px, py = self.chip(h, delta if axis == 0 else 0, delta if axis == 1 else 0)
        there = ((da - delta) % 4, db) if axis == 0 else (da, (db - delta) % 4)
        ref = self.piece(h, da, db, half)
        return pltpu.make_async_remote_copy(
            src_ref=ref,
            dst_ref=ref,
            send_sem=self.send_sem,
            recv_sem=self.recv_sem.at[h, there[0], there[1], half or 0],
            device_id=(self.z, (px * 4 + py) * 2 + self.c),
            device_id_type=MESH,
        )

    def wait(self, h, da, db, half=None):
        ref = self.piece(h, da, db, half)
        pltpu.make_async_copy(ref, ref, self.recv_sem.at[h, da, db, half or 0]).wait()

    def across(self, h, da):
        for delta in (1, -1):
            self.copy(h, da, 0, None, 1, delta).start()

    def begin(self, h):
        for delta in (1, -1):
            self.copy(h, 0, 0, None, 0, delta).start()
        self.across(h, 0)

    def middle(self):
        for da, half, delta in ((3, 0, 1), (1, 1, -1)):
            for h in (0, 1):
                self.wait(h, da, 0)
                self.copy(h, da, 0, half, 0, delta).start()
                self.across(h, da)
        self.turn(0)
        for h in (0, 1):
            self.wait(h, 2, 0, 0)
            self.wait(h, 2, 0, 1)
            self.across(h, 2)
        self.turn(3)
        self.turn(1)
        self.turn(2)

    def turn(self, da):
        for db, half, delta in ((3, 0, 1), (1, 1, -1)):
            for h in (0, 1):
                self.wait(h, da, db)
                self.copy(h, da, db, half, 1, delta).start()

    def end(self):
        for da in (0, 3, 1, 2):
            for h in (0, 1):
                self.wait(h, da, 2, 0)
                self.wait(h, da, 2, 1)

    def sent(self):
        ref = self.buf.at[pl.ds(0, 960)]
        pltpu.make_async_copy(ref, ref, self.send_sem).wait()


class Column:
    def __init__(self, src, dst, sems, place):
        self.src, self.dst, self.sems = src, dst, sems
        self.z, self.chip, self.c = place

    def copy(self, zd, e):
        return pltpu.make_async_remote_copy(
            src_ref=self.src.at[chunk((2 * zd + e) * 16, 16)],
            dst_ref=self.dst.at[chunk((2 * self.z + self.c) * 16, 16)],
            send_sem=self.sems.at[0],
            recv_sem=self.sems.at[1],
            device_id=(zd, 2 * self.chip + e),
            device_id_type=MESH,
        )

    def start(self):
        def step(j, carry):
            for zd in ((self.z + PLANES // 2 - j) % PLANES, (self.z + PLANES // 2 + j) % PLANES):
                for e in (0, 1):
                    self.copy(zd, e).start()
            return carry

        for e in (0, 1):
            self.copy((self.z + PLANES // 2) % PLANES, e).start()
        lax.fori_loop(1, PLANES // 2, step, 0)
        self.copy(self.z, 1 - self.c).start()
        own = chunk((2 * self.z + self.c) * 16, 16)
        self.dst[own, :] = self.src[own, :]

    def wait(self, which):
        ref = self.dst.at[pl.ds(0, 31 * 16)]
        pltpu.make_async_copy(ref, ref, self.sems.at[which]).wait()


FAR_FIRST = sorted(
    ((dx, dy, dc) for dx in range(4) for dy in range(4) for dc in range(2) if (dx, dy, dc) != (0, 0, 0)),
    key=lambda d: -min(d[0], 4 - d[0]) - min(d[1], 4 - d[1]),
)


class Plane:
    def __init__(self, src, dst, sems, place):
        self.src, self.dst, self.sems = src, dst, sems
        self.z, self.o = place

    def start(self):
        x, y, c = self.o // 8, self.o // 2 % 4, self.o % 2
        for dx, dy, dc in FAR_FIRST:
            there = (((x + dx) % 4) * 4 + (y + dy) % 4) * 2 + (c + dc) % 2
            pltpu.make_async_remote_copy(
                src_ref=self.src.at[chunk(there * 32, 32)],
                dst_ref=self.dst.at[chunk(self.o * 32, 32)],
                send_sem=self.sems.at[0],
                recv_sem=self.sems.at[1],
                device_id=(self.z, there),
                device_id_type=MESH,
            ).start()
        own = chunk(self.o * 32, 32)
        self.dst[own, :] = self.src[own, :]

    def wait(self, which):
        ref = self.dst.at[pl.ds(0, 31 * 32)]
        pltpu.make_async_copy(ref, ref, self.sems.at[which]).wait()


def kernel(
    owner_hbm, slot_hbm, g_hbm, lroot_hbm, rroot_hbm,
    arrived_ref,
    owner_ref, slot_ref, g, lroot, rroot, perm, parts, from_left, from_right, swapped, block,
    roots_out, roots_in, blocks_out, blocks_in, lsel, rheld, rfull,
    rows64, zout, zin, stats_out, stats_held, to_blocks, to_places,
    load_sem, near_sem, rs_send, right_sem, left_sem, swap_sem, block_send, block_recv, rheld_send, rheld_recv,
    a1_sem, a2_sem, z_sem, f_sem,
):
    z, o = lax.axis_index("dp"), lax.axis_index("owner")
    chip, c = o // 2, o % 2
    x, y = chip // 4, chip % 4

    loads = [
        pltpu.make_async_copy(src, dst, load_sem.at[n])
        for n, (src, dst) in enumerate(
            ((g_hbm.at[0], g), (lroot_hbm, lroot), (rroot_hbm, rroot), (owner_hbm, owner_ref), (slot_hbm, slot_ref))
        )
    ]
    for load in loads:
        load.start()

    def core_of(dx, dy, dc):
        return (z, (((x + dx) % 4) * 4 + (y + dy) % 4) * 2 + (c + dc) % 2)

    barrier = pltpu.get_barrier_semaphore()
    along_x = [core_of(d, 0, dc) for d in (1, 2, 3) for dc in (0, 1)]
    along_y = [core_of(0, d, dc) for d in (1, 2, 3) for dc in (0, 1)]
    greeted = [((z + 1) % PLANES, o), ((z + PLANES - 1) % PLANES, o), core_of(0, 0, 1)] + along_x + along_y
    for there in greeted:
        pl.semaphore_signal(barrier, inc=1, device_id=there, device_id_type=MESH)

    for n, source in enumerate(SHUFFLES):
        perm[n] = shuffle(source)

    loads[0].wait()
    for h in range(2):
        for q in range(2):
            for w in range(4):
                columns = [(16 * q + r) * WIDTH + 256 * w for r in range(16)]
                stacked = jnp.concatenate([g[16 * h : 16 * h + 16, n : n + 256] for n in columns], axis=0)
                turned = mix(perm[T16], stacked)
                for b in range(16):
                    at = (b % 2) * 32 + 16 * q
                    parts[8 * h + b // 2, at : at + 16, 256 * w : 256 * w + 256] = turned[16 * b : 16 * b + 16]

    pl.semaphore_wait(barrier, len(greeted))

    def rs_copy(right, s, sub):
        rows = pl.ds(sub * 16, 16)
        held = from_left if right else from_right
        part = (z + 8 - s) % PLANES if right else (z + 8 + s) % PLANES
        sems = right_sem if right else left_sem
        return pltpu.make_async_remote_copy(
            src_ref=parts.at[part, rows] if s == rs_first(right, sub) else held.at[s - 1, rows],
            dst_ref=held.at[s, rows],
            send_sem=rs_send,
            recv_sem=sems.at[s, sub],
            device_id=((z + (1 if right else PLANES - 1)) % PLANES, o),
            device_id_type=MESH,
        )

    def rs_first(right, sub):
        return 0 if (sub < SUBS // 2) == right else 1

    def rs_step(s):
        for sub in range(SUBS):
            for right in (True, False):
                if s < rs_first(right, sub):
                    continue
                if s > rs_first(right, sub):
                    rs_copy(right, s - 1, sub).wait_recv()
                    rows = pl.ds(sub * 16, 16)
                    held = from_left if right else from_right
                    part = (z + 8 - s) % PLANES if right else (z + 8 + s) % PLANES
                    total = held[s - 1, rows, :].astype(F32) + parts[part, rows, :].astype(F32)
                    held[s - 1, rows, :] = total.astype(BF16)
                rs_copy(right, s, sub).start()

    rs_step(0)
    rs_step(1)

    for there in along_x:
        pl.semaphore_signal(near_sem, inc=1, device_id=there, device_id_type=MESH)
    loads[1].wait()
    loads[2].wait()
    for k in range(4):
        stacked = jnp.concatenate(
            [
                root[p, 16 * k : 16 * k + 16, 256 * q : 256 * q + 256]
                for p in range(2)
                for root in (lroot, rroot)
                for q in range(4)
            ],
            axis=0,
        )
        roots_out[256 * k : 256 * k + 256, :] = mix(perm[ROOTS_OUT], stacked)
    pl.semaphore_wait(near_sem, len(along_x))
    a1 = Plane(roots_out, roots_in, a1_sem, (z, o))
    a1.start()

    rs_step(2)

    loads[3].wait()
    loads[4].wait()
    places = [owner_ref[b] * 2 + slot_ref[b] for b in range(BLOCKS)]
    row, column = iotas(16, WIDTH)
    for b in range(BLOCKS):
        to_blocks[16 * b : 16 * b + 16, :] = one_hot(column == places[b] * 16 + row)
    column = lax.broadcasted_iota(jnp.int32, (1, 512), 1)
    target = jnp.zeros((1, 512), jnp.int32)
    for b in range(BLOCKS):
        target = jnp.where(column // 16 == b, places[b] * 16, target)
    target = target + column % 16
    for k in range(4):
        row = lax.broadcasted_iota(jnp.int32, (256, 512), 0) + 256 * k
        to_places[256 * k : 256 * k + 256, :] = one_hot(row == target)

    rs_step(3)
    rs_step(4)
    rs_step(5)

    a1.wait(1)
    blocks_out[...] = mix(to_blocks[...], roots_in[...])

    rs_step(6)
    rs_step(7)

    def last_sum(which):
        rows = chunk(which * 32, 32)
        for held, sems in ((from_left, right_sem), (from_right, left_sem)):
            for n in range(2):
                ref = held.at[7, chunk(which * 32 + n * 16, 16)]
                pltpu.make_async_copy(ref, ref, sems.at[7, which * 2 + n]).wait()
        total = parts[z, rows, :].astype(F32) + from_left[7, rows, :].astype(F32) + from_right[7, rows, :].astype(F32)
        return total.astype(BF16)

    def swap_copy(rows_of):
        return pltpu.make_async_remote_copy(
            src_ref=swapped,
            dst_ref=block.at[chunk(rows_of * 32, 32)],
            send_sem=swap_sem.at[0],
            recv_sem=swap_sem.at[1],
            device_id=(z, 2 * chip + 1 - c),
            device_id_type=MESH,
        )

    swapped[...] = last_sum(1 - c)
    swap_copy(o).start()
    block[chunk(o * 32, 32), :] = last_sum(c)
    spread = Spread(block, block_send, block_recv, (z, x, y, c))
    spread.begin(0)
    swap_copy(2 * chip + 1 - c).wait_recv()
    spread.begin(1)
    a2 = Column(blocks_out, blocks_in, a2_sem, (z, chip, c))
    a2.start()
    spread.middle()

    a2.wait(1)
    for h in range(2):
        turned = mix(perm[ROOTS_IN], blocks_in[256 * h : 256 * h + 256, :])
        for q in range(4):
            lsel[32 * h : 32 * h + 32, 256 * q : 256 * q + 256] = turned[32 * q : 32 * q + 32]
            rheld[chunk(chip * 64 + 32 * h, 32), 256 * q : 256 * q + 256] = turned[128 + 32 * q : 160 + 32 * q]
    rspread = Spread(rheld, rheld_send, rheld_recv, (z, x, y, c))
    rspread.begin(0)
    rspread.begin(1)

    spread.end()

    def send_rows(n, product):
        for q in range(4):
            rows64[n, :, 256 * q : 256 * q + 256] = product(q).astype(BF16)
        for h in range(2):
            stacked = jnp.concatenate(
                [rows64[n, 32 * h : 32 * h + 32, 128 * q : 128 * q + 128] for q in range(8)], axis=0
            )
            zout[n, 256 * h : 256 * h + 256, :] = mix(perm[RESULTS_OUT], stacked)
        exchange = Column(zout.at[n], zin.at[n], z_sem.at[n], (z, chip, c))
        exchange.start()
        return exchange

    m, k = iotas(64, 256)
    chosen = one_hot(k == (m >> 2) * 16 + 4 * y + (m & 3))
    stacked = jnp.concatenate([block[chunk(64 * zz + 16 * x, 16), :] for zz in range(PLANES)], axis=0)
    lhs = mix(chosen, stacked)
    zl = send_rows(0, lambda q: times_transposed(lhs, block[256 * q : 256 * q + 256, :]))
    m, k = iotas(64, WIDTH)
    chosen = one_hot(k == (m >> 2) * 64 + 4 * chip + (m & 3))
    columns = jnp.concatenate(
        [times_transposed(chosen, block[256 * q : 256 * q + 256, :]).astype(BF16) for q in range(4)], axis=1
    )
    zr = send_rows(1, lambda q: jnp.dot(columns, block[:, 256 * q : 256 * q + 256], preferred_element_type=F32))

    rspread.middle()
    scaled = jnp.concatenate([mix(lsel[...], block[:, 256 * q : 256 * q + 256]) for q in range(4)], axis=1)

    def to_owners(n, exchange):
        exchange.wait(1)
        stats_out[n] = mix(to_places[...], zin[n])
        owners = Plane(stats_out.at[n], stats_held.at[n], f_sem.at[n], (z, o))
        owners.start()
        return owners

    fl = to_owners(0, zl)

    rspread.end()
    for n in range(4):
        turned = mix(perm[RIGHT_ROWS], rheld[256 * n : 256 * n + 256, :])
        for zz in range(PLANES):
            rfull[64 * zz + 16 * n : 64 * zz + 16 * n + 16, :] = turned[16 * zz : 16 * zz + 16]
    zp = send_rows(2, lambda q: jnp.dot(scaled, rfull[:, 256 * q : 256 * q + 256], preferred_element_type=F32))

    fr = to_owners(1, zr)

    fl.wait(1)
    stores = [pltpu.make_async_copy(stats_held.at[0], arrived_ref.at[pl.ds(0, 1024)], load_sem.at[0])]
    stores[0].start()
    fr.wait(1)
    stores.append(pltpu.make_async_copy(stats_held.at[1], arrived_ref.at[pl.ds(1024, 1024)], load_sem.at[1]))
    stores[1].start()
    zp.wait(1)
    stores.append(pltpu.make_async_copy(zin.at[2], arrived_ref.at[pl.ds(2048, 512)], load_sem.at[2]))
    stores[2].start()

    ref = parts.at[pl.ds(0, 15)]
    pltpu.make_async_copy(ref, ref, rs_send).wait()
    swap_copy(o).wait_send()
    spread.sent()
    rspread.sent()
    for exchange in (a1, a2, zl, zr, zp, fl, fr):
        exchange.wait(0)
    for store in stores:
        store.wait()


def finish(arrived_ref, lstat_ref, rstat_ref, precond_ref, left_ref, right_ref):
    turn = shuffle(transpose16)
    for h in range(2):
        turned = mix(turn, arrived_ref[2048 + 256 * h : 2304 + 256 * h, :])
        for n in range(16):
            precond_ref[16 * h : 16 * h + 16, 128 * n : 128 * n + 128] = turned[16 * n : 16 * n + 16]
    turn = shuffle(stats_in)
    for t, (old, new) in enumerate(((lstat_ref, left_ref), (rstat_ref, right_ref))):
        for k in range(4):
            turned = jnp.dot(turn, arrived_ref[1024 * t + 256 * k : 1024 * t + 256 * k + 256, :], preferred_element_type=F32)
            for p in range(2):
                for n in range(8):
                    at = (p * 8 + n) * 16
                    there = (p, slice(16 * k, 16 * k + 16), slice(128 * n, 128 * n + 128))
                    new[there] = decay_rate * old[there] + (1.0 - decay_rate) * turned[at : at + 16]


def step(grad_partials, block_owner, block_slot, left_stat, right_stat, left_root, right_root):
    vmem = pl.BlockSpec(memory_space=pltpu.VMEM)
    hbm = pl.BlockSpec(memory_space=pl.ANY)
    dma = pltpu.SemaphoreType.DMA
    arrived = pl.pallas_call(
        kernel,
        out_shape=jax.ShapeDtypeStruct((2560, 128), BF16),
        in_specs=[hbm] * 5,
        out_specs=hbm,
        scratch_shapes=[
            pltpu.SMEM((BLOCKS,), jnp.int32),
            pltpu.SMEM((BLOCKS,), jnp.int32),
            pltpu.VMEM((32, 32 * WIDTH), BF16),
            pltpu.VMEM((2, 64, WIDTH), BF16),
            pltpu.VMEM((2, 64, WIDTH), BF16),
            pltpu.VMEM((len(SHUFFLES), 256, 256), BF16),
            pltpu.VMEM((16, 64, WIDTH), BF16),
            pltpu.VMEM((8, 64, WIDTH), BF16),
            pltpu.VMEM((8, 64, WIDTH), BF16),
            pltpu.VMEM((32, WIDTH), BF16),
            pltpu.VMEM((WIDTH, WIDTH), BF16),
            pltpu.VMEM((1024, 256), BF16),
            pltpu.VMEM((1024, 256), BF16),
            pltpu.VMEM((512, 256), BF16),
            pltpu.VMEM((512, 256), BF16),
            pltpu.VMEM((64, WIDTH), BF16),
            pltpu.VMEM((WIDTH, WIDTH), BF16),
            pltpu.VMEM((WIDTH, WIDTH), BF16),
            pltpu.VMEM((3, 64, WIDTH), BF16),
            pltpu.VMEM((3, 512, 128), BF16),
            pltpu.VMEM((3, 512, 128), BF16),
            pltpu.VMEM((2, 1024, 128), BF16),
            pltpu.VMEM((2, 1024, 128), BF16),
            pltpu.VMEM((512, 1024), BF16),
            pltpu.VMEM((1024, 512), BF16),
            dma((5,)),
            pltpu.SemaphoreType.REGULAR,
            dma,
            dma((8, SUBS)),
            dma((8, SUBS)),
            dma((2,)),
            dma,
            dma((2, 4, 4, 2)),
            dma,
            dma((2, 4, 4, 2)),
            dma((2,)),
            dma((2,)),
            dma((3, 2)),
            dma((2, 2)),
        ],
        compiler_params=pltpu.CompilerParams(
            collective_id=0, has_side_effects=True, vmem_limit_bytes=60 * 1024 * 1024
        ),
    )(block_owner, block_slot, grad_partials, left_root, right_root)
    return pl.pallas_call(
        finish,
        out_shape=(
            jax.ShapeDtypeStruct((BLOCKS, 2 * WIDTH), BF16),
            jax.ShapeDtypeStruct(left_stat.shape, F32),
            jax.ShapeDtypeStruct(right_stat.shape, F32),
        ),
        in_specs=[vmem] * 3,
        out_specs=[vmem] * 3,
        compiler_params=pltpu.CompilerParams(vmem_limit_bytes=16 * 1024 * 1024),
    )(arrived, left_stat, right_stat)


def solution(mesh):
    return jax.shard_map(
        step,
        mesh=mesh,
        in_specs=(
            P("dp", None, "owner"),
            P(),
            P(),
            P("owner", "dp", None),
            P("owner", "dp", None),
            P("owner", "dp", None),
            P("owner", "dp", None),
        ),
        out_specs=(P(None, ("dp", "owner")), P("owner", "dp", None), P("owner", "dp", None)),
        check_vma=False,
    )
```

```python
import functools

import jax
import jax.numpy as jnp
from jax import lax
from jax.experimental import pallas as pl
from jax.experimental.pallas import tpu as pltpu
from jax.sharding import PartitionSpec as P

decay_rate = 0.95

MESH = pl.DeviceIdType.MESH
BF16 = jnp.bfloat16
F32 = jnp.float32
PLANES = 16
OWNERS = 32
BLOCKS = 32
WIDTH = 1024
SUBS = 4


def iotas(rows, columns):
    return (
        lax.broadcasted_iota(jnp.int32, (rows, columns), 0),
        lax.broadcasted_iota(jnp.int32, (rows, columns), 1),
    )


def one_hot(hit):
    return jnp.where(hit, 1.0, 0.0).astype(BF16)


def mix(chooser, data):
    return jnp.dot(chooser, data, preferred_element_type=F32).astype(BF16)


def times_transposed(a, b):
    return lax.dot_general(a, b, (((1,), (1,)), ((), ())), preferred_element_type=F32)


def chunk(start, size, unit=None):
    return pl.ds(pl.multiple_of(start, unit or size), size)


def transpose16(m):
    return (m % 16) * 16 + m // 16


def roots_out(m):
    return (((m >> 4) & 1) * 8 + (m & 7)) * 16 + (m >> 5) * 2 + ((m >> 3) & 1)


def results_in(m):
    return ((m >> 1) & 15) * 16 + (m & 1) * 8 + (m >> 5)


def results_out(m):
    return ((m & 7) * 16 + (m >> 4)) * 2 + ((m >> 3) & 1)


def stats_in(m):
    return ((m >> 1) & 7) * 32 + (m >> 7) * 16 + (m & 1) * 8 + ((m >> 4) & 7)


def shuffle(source):
    m, k = iotas(256, 256)
    return one_hot(k == source(m))


SHUFFLES = (transpose16, roots_out, results_in, results_out)
T16, ROOTS_OUT, RESULTS_IN, RESULTS_OUT = range(4)


class Spread:
    def __init__(self, buf, send_sem, recv_sem, place):
        self.buf, self.send_sem, self.recv_sem = buf, send_sem, recv_sem
        self.z, self.x, self.y, self.c = place

    def chip(self, h, da, db):
        first, second = (self.x, self.y) if h == 0 else (self.y, self.x)
        first, second = (first + da) % 4, (second + db) % 4
        return (first, second) if h == 0 else (second, first)

    def piece(self, h, da, db, half=None):
        px, py = self.chip(h, da, db)
        start = px * 256 + py * 64 + (self.c if h == 0 else 1 - self.c) * 32
        if half is None:
            return self.buf.at[chunk(start, 32)]
        return self.buf.at[chunk(start + 16 * half, 16)]

    def copy(self, h, da, db, half, axis, delta):
        px, py = self.chip(h, delta if axis == 0 else 0, delta if axis == 1 else 0)
        there = ((da - delta) % 4, db) if axis == 0 else (da, (db - delta) % 4)
        ref = self.piece(h, da, db, half)
        return pltpu.make_async_remote_copy(
            src_ref=ref,
            dst_ref=ref,
            send_sem=self.send_sem,
            recv_sem=self.recv_sem.at[h, there[0], there[1], half or 0],
            device_id=(self.z, (px * 4 + py) * 2 + self.c),
            device_id_type=MESH,
        )

    def wait(self, h, da, db, half=None):
        ref = self.piece(h, da, db, half)
        pltpu.make_async_copy(ref, ref, self.recv_sem.at[h, da, db, half or 0]).wait()

    def across(self, h, da):
        for delta in (1, -1):
            self.copy(h, da, 0, None, 1, delta).start()

    def begin(self, h):
        for delta in (1, -1):
            self.copy(h, 0, 0, None, 0, delta).start()
        self.across(h, 0)

    def early(self):
        for da, half, delta in ((3, 0, 1), (1, 1, -1)):
            for h in (0, 1):
                self.wait(h, da, 0)
                self.copy(h, da, 0, half, 0, delta).start()
                self.across(h, da)

    def middle(self):
        self.turn(0)
        for h in (0, 1):
            self.wait(h, 2, 0, 0)
            self.wait(h, 2, 0, 1)
            self.copy(h, 2, 0, None, 1, 2).start()
            self.across(h, 2)

    def late(self):
        self.turn(3)
        self.turn(1)

    def turn(self, da):
        for db, half, delta in ((3, 0, 1), (1, 1, -1)):
            for h in (0, 1):
                self.wait(h, da, db)
                self.copy(h, da, db, half, 1, delta).start()

    def end(self):
        for da in (0, 3, 1):
            for h in (0, 1):
                self.wait(h, da, 2, 0)
                self.wait(h, da, 2, 1)
        for db in (3, 1, 2):
            for h in (0, 1):
                self.wait(h, 2, db)

    def sent(self):
        ref = self.buf.at[pl.ds(0, 960)]
        pltpu.make_async_copy(ref, ref, self.send_sem).wait()


class Column:
    def __init__(self, src, dst, sems, place):
        self.src, self.dst, self.sems = src, dst, sems
        self.z, self.chip, self.c = place

    def copy(self, zd, e):
        return pltpu.make_async_remote_copy(
            src_ref=self.src.at[chunk((2 * zd + e) * 16, 16)],
            dst_ref=self.dst.at[chunk((2 * self.z + self.c) * 16, 16)],
            send_sem=self.sems.at[0],
            recv_sem=self.sems.at[1],
            device_id=(zd, 2 * self.chip + e),
            device_id_type=MESH,
        )

    def start(self):
        def step(j, carry):
            for zd in ((self.z + PLANES // 2 - j) % PLANES, (self.z + PLANES // 2 + j) % PLANES):
                for e in (0, 1):
                    self.copy(zd, e).start()
            return carry

        for e in (0, 1):
            self.copy((self.z + PLANES // 2) % PLANES, e).start()
        lax.fori_loop(1, PLANES // 2, step, 0)
        self.copy(self.z, 1 - self.c).start()
        own = chunk((2 * self.z + self.c) * 16, 16)
        self.dst[own, :] = self.src[own, :]

    def wait(self, which):
        ref = self.dst.at[pl.ds(0, 31 * 16)]
        pltpu.make_async_copy(ref, ref, self.sems.at[which]).wait()


FAR_FIRST = sorted(
    ((dx, dy, dc) for dx in range(4) for dy in range(4) for dc in range(2) if (dx, dy, dc) != (0, 0, 0)),
    key=lambda d: -min(d[0], 4 - d[0]) - min(d[1], 4 - d[1]),
)


class Plane:
    def __init__(self, src, dst, sems, place):
        self.src, self.dst, self.sems = src, dst, sems
        self.z, self.o = place

    def start(self):
        x, y, c = self.o // 8, self.o // 2 % 4, self.o % 2
        for dx, dy, dc in FAR_FIRST:
            there = (((x + dx) % 4) * 4 + (y + dy) % 4) * 2 + (c + dc) % 2
            pltpu.make_async_remote_copy(
                src_ref=self.src.at[chunk(there * 32, 32)],
                dst_ref=self.dst.at[chunk(self.o * 32, 32)],
                send_sem=self.sems.at[0],
                recv_sem=self.sems.at[1],
                device_id=(self.z, there),
                device_id_type=MESH,
            ).start()
        own = chunk(self.o * 32, 32)
        self.dst[own, :] = self.src[own, :]

    def wait(self, which):
        ref = self.dst.at[pl.ds(0, 31 * 32)]
        pltpu.make_async_copy(ref, ref, self.sems.at[which]).wait()


def kernel(
    owner_hbm, slot_hbm, g_hbm, lroot_hbm, rroot_hbm,
    arrived_ref,
    owner_ref, slot_ref, g, lroot, rroot, perm, parts, from_left, from_right, swapped, block,
    roots_out, roots_in, blocks_out, blocks_in, lsel, rheld, order,
    rows64, zout, zin, stats_out, to_blocks, to_places,
    load_sem, near_sem, rs_send, right_sem, left_sem, swap_sem, block_send, block_recv, rheld_send, rheld_recv,
    a1_sem, a2_sem, z_sem, f_sem,
):
    z, o = lax.axis_index("dp"), lax.axis_index("owner")
    chip, c = o // 2, o % 2
    x, y = chip // 4, chip % 4

    def core_of(dx, dy, dc):
        return (z, (((x + dx) % 4) * 4 + (y + dy) % 4) * 2 + (c + dc) % 2)

    barrier = pltpu.get_barrier_semaphore()
    along_x = [core_of(d, 0, dc) for d in (1, 2, 3) for dc in (0, 1)]
    along_y = [core_of(0, d, dc) for d in (1, 2, 3) for dc in (0, 1)]
    greeted = [((z + 1) % PLANES, o), ((z + PLANES - 1) % PLANES, o), core_of(0, 0, 1)] + along_x + along_y
    for there in greeted:
        pl.semaphore_signal(barrier, inc=1, device_id=there, device_id_type=MESH)

    first_half = (z + 8) % PLANES // 8
    halves = [chunk(16 * h, 16) for h in (first_half, 1 - first_half)]
    loads = [
        pltpu.make_async_copy(src, dst, load_sem.at[n])
        for n, (src, dst) in enumerate(
            ((g_hbm.at[0, halves[0]], g.at[halves[0]]), (g_hbm.at[0, halves[1]], g.at[halves[1]]), (lroot_hbm, lroot), (rroot_hbm, rroot), (owner_hbm, owner_ref), (slot_hbm, slot_ref))
        )
    ]
    for load in loads:
        load.start()

    perm[T16] = shuffle(transpose16)

    def make_parts(h):
        for q in range(2):
            for w in range(4):
                columns = [(16 * q + r) * WIDTH + 256 * w for r in range(16)]
                stacked = jnp.concatenate([g[chunk(16 * h, 16), n : n + 256] for n in columns], axis=0)
                turned = mix(perm[T16], stacked)
                for b in range(16):
                    at = (b % 2) * 32 + 16 * q
                    parts[8 * h + b // 2, at : at + 16, 256 * w : 256 * w + 256] = turned[16 * b : 16 * b + 16]

    loads[0].wait()
    make_parts(first_half)
    pl.semaphore_wait(barrier, len(greeted))

    def rs_copy(right, s, sub):
        rows = pl.ds(sub * 16, 16)
        held = from_left if right else from_right
        part = (z + 8 - s) % PLANES if right else (z + 8 + s) % PLANES
        sems = right_sem if right else left_sem
        return pltpu.make_async_remote_copy(
            src_ref=parts.at[part, rows] if s == rs_first(right, sub) else held.at[s - 1, rows],
            dst_ref=held.at[s, rows],
            send_sem=rs_send,
            recv_sem=sems.at[s, sub],
            device_id=((z + (1 if right else PLANES - 1)) % PLANES, o),
            device_id_type=MESH,
        )

    def rs_first(right, sub):
        return 0 if (sub < SUBS // 2) == right else 1

    def rs_step(s):
        for sub in range(SUBS):
            for right in (True, False):
                if s < rs_first(right, sub):
                    continue
                if s > rs_first(right, sub):
                    rs_copy(right, s - 1, sub).wait_recv()
                    rows = pl.ds(sub * 16, 16)
                    held = from_left if right else from_right
                    part = (z + 8 - s) % PLANES if right else (z + 8 + s) % PLANES
                    total = held[s - 1, rows, :].astype(F32) + parts[part, rows, :].astype(F32)
                    held[s - 1, rows, :] = total.astype(BF16)
                rs_copy(right, s, sub).start()

    rs_step(0)
    loads[1].wait()
    make_parts(1 - first_half)
    rs_step(1)
    for n, source in enumerate(SHUFFLES[1:]):
        perm[n + 1] = shuffle(source)

    for there in along_x:
        pl.semaphore_signal(near_sem, inc=1, device_id=there, device_id_type=MESH)
    loads[2].wait()
    loads[3].wait()
    for n, root in enumerate((rroot, lroot)):
        for k in range(4):
            stacked = jnp.concatenate(
                [root[p, 16 * k : 16 * k + 16, 128 * q : 128 * q + 128] for p in range(2) for q in range(8)], axis=0
            )
            roots_out[n, 256 * k : 256 * k + 256, :] = mix(perm[ROOTS_OUT], stacked)
    pl.semaphore_wait(near_sem, len(along_x))
    a1 = [Plane(roots_out.at[n], roots_in.at[n], a1_sem.at[n], (z, o)) for n in range(2)]
    for exchange in a1:
        exchange.start()

    rs_step(2)

    loads[4].wait()
    loads[5].wait()
    places = [owner_ref[b] * 2 + slot_ref[b] for b in range(BLOCKS)]
    row, column = iotas(16, WIDTH)
    for b in range(BLOCKS):
        to_blocks[16 * b : 16 * b + 16, :] = one_hot(column == places[b] * 16 + row)
    column = lax.broadcasted_iota(jnp.int32, (1, 512), 1)
    target = jnp.zeros((1, 512), jnp.int32)
    for b in range(BLOCKS):
        target = jnp.where(column // 16 == b, places[b] * 16, target)
    target = target + column % 16
    for k in range(4):
        row = lax.broadcasted_iota(jnp.int32, (256, 512), 0) + 256 * k
        to_places[256 * k : 256 * k + 256, :] = one_hot(row == target)

    rs_step(3)

    for q in range(4):
        row, column = iotas(WIDTH, 256)
        chosen = ((column >> 2) & 15) * 64 + 16 * q + ((column >> 6) & 3) * 4 + (column & 3)
        order[:, 256 * q : 256 * q + 256] = one_hot(row == chosen)

    rs_step(4)
    rs_step(5)

    for n in range(2):
        a1[n].wait(1)
        blocks_out[n] = mix(to_blocks[...], roots_in[n])

    rs_step(6)
    rs_step(7)

    def last_sum(which):
        rows = chunk(which * 32, 32)
        for held, sems in ((from_left, right_sem), (from_right, left_sem)):
            for n in range(2):
                ref = held.at[7, chunk(which * 32 + n * 16, 16)]
                pltpu.make_async_copy(ref, ref, sems.at[7, which * 2 + n]).wait()
        total = parts[z, rows, :].astype(F32) + from_left[7, rows, :].astype(F32) + from_right[7, rows, :].astype(F32)
        return total.astype(BF16)

    def swap_copy(rows_of):
        return pltpu.make_async_remote_copy(
            src_ref=swapped,
            dst_ref=block.at[chunk(rows_of * 32, 32)],
            send_sem=swap_sem.at[0],
            recv_sem=swap_sem.at[1],
            device_id=(z, 2 * chip + 1 - c),
            device_id_type=MESH,
        )

    swapped[...] = last_sum(1 - c)
    swap_copy(o).start()
    block[chunk(o * 32, 32), :] = last_sum(c)
    spread = Spread(block, block_send, block_recv, (z, x, y, c))
    spread.begin(0)
    swap_copy(2 * chip + 1 - c).wait_recv()
    spread.begin(1)
    a2 = [Column(blocks_out.at[n], blocks_in.at[n], a2_sem.at[n], (z, chip, c)) for n in range(2)]
    a2[0].start()
    spread.early()
    a2[1].start()
    spread.middle()
    spread.late()

    def rows_of_root(n, held, start):
        a2[n].wait(1)
        for h in range(2):
            turned = mix(perm[RESULTS_IN], blocks_in[n, 256 * h : 256 * h + 256, :])
            for q in range(8):
                held[chunk(start + 32 * h, 32), 128 * q : 128 * q + 128] = turned[32 * q : 32 * q + 32]

    rows_of_root(0, rheld, chip * 64)
    rspread = Spread(rheld, rheld_send, rheld_recv, (z, x, y, c))
    rspread.begin(0)
    rspread.begin(1)
    spread.end()

    def send_rows(n, product):
        for q in range(4):
            rows64[n, :, 256 * q : 256 * q + 256] = product(q).astype(BF16)
        for h in range(2):
            stacked = jnp.concatenate(
                [rows64[n, 32 * h : 32 * h + 32, 128 * q : 128 * q + 128] for q in range(8)], axis=0
            )
            zout[n, 256 * h : 256 * h + 256, :] = mix(perm[RESULTS_OUT], stacked)
        arrive = arrived_ref.at[pl.ds(2048, 512)] if n == 2 else zin.at[n]
        exchange = Column(zout.at[n], arrive, z_sem.at[n], (z, chip, c))
        exchange.start()
        return exchange

    m, k = iotas(64, 256)
    chosen = one_hot(k == (m >> 2) * 16 + 4 * y + (m & 3))
    stacked = jnp.concatenate([block[chunk(64 * zz + 16 * x, 16), :] for zz in range(PLANES)], axis=0)
    lhs = mix(chosen, stacked)
    zl = send_rows(0, lambda q: times_transposed(lhs, block[256 * q : 256 * q + 256, :]))
    m, k = iotas(64, WIDTH)
    chosen = one_hot(k == (m >> 2) * 64 + 4 * chip + (m & 3))
    columns = jnp.concatenate(
        [times_transposed(chosen, block[256 * q : 256 * q + 256, :]).astype(BF16) for q in range(4)], axis=1
    )
    zr = send_rows(1, lambda q: jnp.dot(columns, block[:, 256 * q : 256 * q + 256], preferred_element_type=F32))

    rspread.early()
    rows_of_root(1, lsel, 0)
    rspread.middle()
    scaled = jnp.concatenate([mix(lsel[...], block[:, 256 * q : 256 * q + 256]) for q in range(4)], axis=1)
    scaled = jnp.concatenate([mix(scaled, order[:, 256 * q : 256 * q + 256]) for q in range(4)], axis=1)
    rspread.late()

    rspread.end()
    zp = send_rows(2, lambda q: jnp.dot(scaled, rheld[:, 256 * q : 256 * q + 256], preferred_element_type=F32))

    def to_owners(n, exchange):
        exchange.wait(1)
        stats_out[n] = mix(to_places[...], zin[n])
        owners = Plane(stats_out.at[n], arrived_ref.at[pl.ds(1024 * n, 1024)], f_sem.at[n], (z, o))
        owners.start()
        return owners

    fl = to_owners(0, zl)
    fr = to_owners(1, zr)

    for exchange in (fl, fr, zp):
        exchange.wait(1)

    ref = parts.at[pl.ds(0, 15)]
    pltpu.make_async_copy(ref, ref, rs_send).wait()
    swap_copy(o).wait_send()
    spread.sent()
    rspread.sent()
    for exchange in (*a1, *a2, zl, zr, zp, fl, fr):
        exchange.wait(0)


def finish(arrived_ref, lstat_ref, rstat_ref, precond_ref, left_ref, right_ref):
    turn = shuffle(transpose16)
    for h in range(2):
        turned = mix(turn, arrived_ref[2048 + 256 * h : 2304 + 256 * h, :])
        for n in range(16):
            precond_ref[16 * h : 16 * h + 16, 128 * n : 128 * n + 128] = turned[16 * n : 16 * n + 16]
    turn = shuffle(stats_in)
    for t, (old, new) in enumerate(((lstat_ref, left_ref), (rstat_ref, right_ref))):
        for k in range(4):
            turned = jnp.dot(turn, arrived_ref[1024 * t + 256 * k : 1024 * t + 256 * k + 256, :], preferred_element_type=F32)
            for p in range(2):
                for n in range(8):
                    at = (p * 8 + n) * 16
                    there = (p, slice(16 * k, 16 * k + 16), slice(128 * n, 128 * n + 128))
                    new[there] = decay_rate * old[there] + (1.0 - decay_rate) * turned[at : at + 16]


def step(grad_partials, block_owner, block_slot, left_stat, right_stat, left_root, right_root):
    vmem = pl.BlockSpec(memory_space=pltpu.VMEM)
    hbm = pl.BlockSpec(memory_space=pl.ANY)
    dma = pltpu.SemaphoreType.DMA
    arrived = pl.pallas_call(
        kernel,
        out_shape=jax.ShapeDtypeStruct((2560, 128), BF16),
        in_specs=[hbm] * 5,
        out_specs=vmem,
        scratch_shapes=[
            pltpu.SMEM((BLOCKS,), jnp.int32),
            pltpu.SMEM((BLOCKS,), jnp.int32),
            pltpu.VMEM((32, 32 * WIDTH), BF16),
            pltpu.VMEM((2, 64, WIDTH), BF16),
            pltpu.VMEM((2, 64, WIDTH), BF16),
            pltpu.VMEM((len(SHUFFLES), 256, 256), BF16),
            pltpu.VMEM((16, 64, WIDTH), BF16),
            pltpu.VMEM((8, 64, WIDTH), BF16),
            pltpu.VMEM((8, 64, WIDTH), BF16),
            pltpu.VMEM((32, WIDTH), BF16),
            pltpu.VMEM((WIDTH, WIDTH), BF16),
            pltpu.VMEM((2, 1024, 128), BF16),
            pltpu.VMEM((2, 1024, 128), BF16),
            pltpu.VMEM((2, 512, 128), BF16),
            pltpu.VMEM((2, 512, 128), BF16),
            pltpu.VMEM((64, WIDTH), BF16),
            pltpu.VMEM((WIDTH, WIDTH), BF16),
            pltpu.VMEM((WIDTH, WIDTH), BF16),
            pltpu.VMEM((3, 64, WIDTH), BF16),
            pltpu.VMEM((3, 512, 128), BF16),
            pltpu.VMEM((2, 512, 128), BF16),
            pltpu.VMEM((2, 1024, 128), BF16),
            pltpu.VMEM((512, 1024), BF16),
            pltpu.VMEM((1024, 512), BF16),
            dma((6,)),
            pltpu.SemaphoreType.REGULAR,
            dma,
            dma((8, SUBS)),
            dma((8, SUBS)),
            dma((2,)),
            dma,
            dma((2, 4, 4, 2)),
            dma,
            dma((2, 4, 4, 2)),
            dma((2, 2)),
            dma((2, 2)),
            dma((3, 2)),
            dma((2, 2)),
        ],
        compiler_params=pltpu.CompilerParams(
            collective_id=0, has_side_effects=True, vmem_limit_bytes=60 * 1024 * 1024
        ),
    )(block_owner, block_slot, grad_partials, left_root, right_root)
    return pl.pallas_call(
        finish,
        out_shape=(
            jax.ShapeDtypeStruct((BLOCKS, 2 * WIDTH), BF16),
            jax.ShapeDtypeStruct(left_stat.shape, F32),
            jax.ShapeDtypeStruct(right_stat.shape, F32),
        ),
        in_specs=[vmem] * 3,
        out_specs=[vmem] * 3,
        compiler_params=pltpu.CompilerParams(vmem_limit_bytes=16 * 1024 * 1024),
    )(arrived, left_stat, right_stat)


def solution(mesh):
    return jax.shard_map(
        step,
        mesh=mesh,
        in_specs=(
            P("dp", None, "owner"),
            P(),
            P(),
            P("owner", "dp", None),
            P("owner", "dp", None),
            P("owner", "dp", None),
            P("owner", "dp", None),
        ),
        out_specs=(P(None, ("dp", "owner")), P("owner", "dp", None), P("owner", "dp", None)),
        check_vma=False,
    )
```

```python
import functools

import jax
import jax.numpy as jnp
from jax import lax
from jax.experimental import pallas as pl
from jax.experimental.pallas import tpu as pltpu
from jax.sharding import PartitionSpec as P

decay_rate = 0.95

MESH = pl.DeviceIdType.MESH
BF16 = jnp.bfloat16
F32 = jnp.float32
PLANES = 16
OWNERS = 32
BLOCKS = 32
WIDTH = 1024
SUBS = 4


def iotas(rows, columns):
    return (
        lax.broadcasted_iota(jnp.int32, (rows, columns), 0),
        lax.broadcasted_iota(jnp.int32, (rows, columns), 1),
    )


def one_hot(hit):
    return jnp.where(hit, 1.0, 0.0).astype(BF16)


def mix(chooser, data):
    return jnp.dot(chooser, data, preferred_element_type=F32).astype(BF16)


def times_transposed(a, b):
    return lax.dot_general(a, b, (((1,), (1,)), ((), ())), preferred_element_type=F32)


def chunk(start, size, unit=None):
    return pl.ds(pl.multiple_of(start, unit or size), size)


def transpose16(m):
    return (m % 16) * 16 + m // 16


def roots_out_rows(m):
    return (((m >> 4) & 1) * 8 + (m & 7)) * 16 + (m >> 5) * 2 + ((m >> 3) & 1)


def results_in(m):
    return ((m >> 1) & 15) * 16 + (m & 1) * 8 + (m >> 5)


def results_out(m):
    return ((m & 7) * 16 + (m >> 4)) * 2 + ((m >> 3) & 1)


def stats_in(m):
    return ((m >> 1) & 7) * 32 + (m >> 7) * 16 + (m & 1) * 8 + ((m >> 4) & 7)


def shuffle(source):
    m, k = iotas(256, 256)
    return one_hot(k == source(m))


T16, ROOTS_OUT, RESULTS_IN, RESULTS_OUT = range(4)


class Spread:
    def __init__(self, buf, send_sem, recv_sem, place):
        self.buf, self.send_sem, self.recv_sem = buf, send_sem, recv_sem
        self.z, self.x, self.y, self.c = place

    def chip(self, h, da, db):
        first, second = (self.x, self.y) if h == 0 else (self.y, self.x)
        first, second = (first + da) % 4, (second + db) % 4
        return (first, second) if h == 0 else (second, first)

    def piece(self, h, da, db, half=None):
        px, py = self.chip(h, da, db)
        start = px * 256 + py * 64 + (self.c if h == 0 else 1 - self.c) * 32
        if half is None:
            return self.buf.at[chunk(start, 32)]
        return self.buf.at[chunk(start + 16 * half, 16)]

    def copy(self, h, da, db, half, axis, delta):
        px, py = self.chip(h, delta if axis == 0 else 0, delta if axis == 1 else 0)
        there = ((da - delta) % 4, db) if axis == 0 else (da, (db - delta) % 4)
        ref = self.piece(h, da, db, half)
        return pltpu.make_async_remote_copy(
            src_ref=ref,
            dst_ref=ref,
            send_sem=self.send_sem,
            recv_sem=self.recv_sem.at[h, there[0], there[1], half or 0],
            device_id=(self.z, (px * 4 + py) * 2 + self.c),
            device_id_type=MESH,
        )

    def wait(self, h, da, db, half=None):
        ref = self.piece(h, da, db, half)
        pltpu.make_async_copy(ref, ref, self.recv_sem.at[h, da, db, half or 0]).wait()

    def across(self, h, da):
        for delta in (1, -1):
            self.copy(h, da, 0, None, 1, delta).start()

    def begin(self, h):
        for delta in (1, -1):
            self.copy(h, 0, 0, None, 0, delta).start()
        self.across(h, 0)

    def early(self):
        for da, half, delta in ((3, 0, 1), (1, 1, -1)):
            for h in (0, 1):
                self.wait(h, da, 0)
                self.copy(h, da, 0, half, 0, delta).start()
                self.across(h, da)

    def middle(self):
        self.turn(0)
        for h in (0, 1):
            self.wait(h, 2, 0, 0)
            self.wait(h, 2, 0, 1)
            self.copy(h, 2, 0, None, 1, 2).start()
            self.across(h, 2)

    def late(self):
        self.turn(3)
        self.turn(1)

    def turn(self, da):
        for db, half, delta in ((3, 0, 1), (1, 1, -1)):
            for h in (0, 1):
                self.wait(h, da, db)
                self.copy(h, da, db, half, 1, delta).start()

    def end(self):
        for da in (0, 3, 1):
            for h in (0, 1):
                self.wait(h, da, 2, 0)
                self.wait(h, da, 2, 1)
        for db in (3, 1, 2):
            for h in (0, 1):
                self.wait(h, 2, db)

    def sent(self):
        ref = self.buf.at[pl.ds(0, 960)]
        pltpu.make_async_copy(ref, ref, self.send_sem).wait()


class Column:
    def __init__(self, src, dst, sems, place):
        self.src, self.dst, self.sems = src, dst, sems
        self.z, self.chip, self.c = place

    def copy(self, zd, e):
        return pltpu.make_async_remote_copy(
            src_ref=self.src.at[chunk((2 * zd + e) * 16, 16)],
            dst_ref=self.dst.at[chunk((2 * self.z + self.c) * 16, 16)],
            send_sem=self.sems.at[0],
            recv_sem=self.sems.at[1],
            device_id=(zd, 2 * self.chip + e),
            device_id_type=MESH,
        )

    def start(self):
        def step(j, carry):
            for zd in ((self.z + PLANES // 2 - j) % PLANES, (self.z + PLANES // 2 + j) % PLANES):
                for e in (0, 1):
                    self.copy(zd, e).start()
            return carry

        for e in (0, 1):
            self.copy((self.z + PLANES // 2) % PLANES, e).start()
        lax.fori_loop(1, PLANES // 2, step, 0)
        self.copy(self.z, 1 - self.c).start()
        own = chunk((2 * self.z + self.c) * 16, 16)
        self.dst[own, :] = self.src[own, :]

    def wait(self, which):
        ref = self.dst.at[pl.ds(0, 31 * 16)]
        pltpu.make_async_copy(ref, ref, self.sems.at[which]).wait()


FAR_FIRST = sorted(
    ((dx, dy, dc) for dx in range(4) for dy in range(4) for dc in range(2) if (dx, dy, dc) != (0, 0, 0)),
    key=lambda d: -min(d[0], 4 - d[0]) - min(d[1], 4 - d[1]),
)


class Plane:
    def __init__(self, src, dst, sems, place):
        self.src, self.dst, self.sems = src, dst, sems
        self.z, self.o = place

    def start(self):
        x, y, c = self.o // 8, self.o // 2 % 4, self.o % 2
        for dx, dy, dc in FAR_FIRST:
            there = (((x + dx) % 4) * 4 + (y + dy) % 4) * 2 + (c + dc) % 2
            pltpu.make_async_remote_copy(
                src_ref=self.src.at[chunk(there * 32, 32)],
                dst_ref=self.dst.at[chunk(self.o * 32, 32)],
                send_sem=self.sems.at[0],
                recv_sem=self.sems.at[1],
                device_id=(self.z, there),
                device_id_type=MESH,
            ).start()
        own = chunk(self.o * 32, 32)
        self.dst[own, :] = self.src[own, :]

    def wait(self, which):
        ref = self.dst.at[pl.ds(0, 31 * 32)]
        pltpu.make_async_copy(ref, ref, self.sems.at[which]).wait()


def kernel(
    owner_hbm, slot_hbm, g_hbm, lroot_hbm, rroot_hbm,
    arrived_ref,
    owner_ref, slot_ref, g, lroot, rroot, perm, parts, from_left, from_right, swapped, block,
    roots_out, roots_in, blocks_out, blocks_in, lsel, rheld, order,
    rows64, zout, zin, stats_out, to_blocks, to_places,
    load_sem, near_sem, rs_send, right_sem, left_sem, swap_sem, block_send, block_recv, rheld_send, rheld_recv,
    a1_sem, a2_sem, z_sem, f_sem,
):
    z, o = lax.axis_index("dp"), lax.axis_index("owner")
    chip, c = o // 2, o % 2
    x, y = chip // 4, chip % 4

    def core_of(dx, dy, dc):
        return (z, (((x + dx) % 4) * 4 + (y + dy) % 4) * 2 + (c + dc) % 2)

    barrier = pltpu.get_barrier_semaphore()
    along_x = [core_of(d, 0, dc) for d in (1, 2, 3) for dc in (0, 1)]
    along_y = [core_of(0, d, dc) for d in (1, 2, 3) for dc in (0, 1)]
    greeted = [((z + 1) % PLANES, o), ((z + PLANES - 1) % PLANES, o), core_of(0, 0, 1)] + along_x + along_y
    for there in greeted:
        pl.semaphore_signal(barrier, inc=1, device_id=there, device_id_type=MESH)

    first_half = (z + 8) % PLANES // 8
    halves = [chunk(16 * h, 16) for h in (first_half, 1 - first_half)]
    loads = [
        pltpu.make_async_copy(src, dst, load_sem.at[n])
        for n, (src, dst) in enumerate(
            ((g_hbm.at[0, halves[0]], g.at[halves[0]]), (g_hbm.at[0, halves[1]], g.at[halves[1]]), (rroot_hbm, rroot), (lroot_hbm, lroot), (owner_hbm, owner_ref), (slot_hbm, slot_ref))
        )
    ]
    for load in loads:
        load.start()

    perm[T16] = shuffle(transpose16)

    def make_parts(h):
        for q in range(2):
            for w in range(4):
                columns = [(16 * q + r) * WIDTH + 256 * w for r in range(16)]
                stacked = jnp.concatenate([g[chunk(16 * h, 16), n : n + 256] for n in columns], axis=0)
                turned = mix(perm[T16], stacked)
                for b in range(16):
                    at = (b % 2) * 32 + 16 * q
                    parts[8 * h + b // 2, at : at + 16, 256 * w : 256 * w + 256] = turned[16 * b : 16 * b + 16]

    loads[0].wait()
    make_parts(first_half)
    pl.semaphore_wait(barrier, len(greeted))

    def rs_copy(right, s, sub):
        rows = pl.ds(sub * 16, 16)
        held = from_left if right else from_right
        part = (z + 8 - s) % PLANES if right else (z + 8 + s) % PLANES
        sems = right_sem if right else left_sem
        return pltpu.make_async_remote_copy(
            src_ref=parts.at[part, rows] if s == rs_first(right, sub) else held.at[s - 1, rows],
            dst_ref=held.at[s, rows],
            send_sem=rs_send,
            recv_sem=sems.at[s, sub],
            device_id=((z + (1 if right else PLANES - 1)) % PLANES, o),
            device_id_type=MESH,
        )

    def rs_first(right, sub):
        return 0 if (sub < SUBS // 2) == right else 1

    def rs_step(s):
        for sub in range(SUBS):
            for right in (True, False):
                if s < rs_first(right, sub):
                    continue
                if s > rs_first(right, sub):
                    rs_copy(right, s - 1, sub).wait_recv()
                    rows = pl.ds(sub * 16, 16)
                    held = from_left if right else from_right
                    part = (z + 8 - s) % PLANES if right else (z + 8 + s) % PLANES
                    total = held[s - 1, rows, :].astype(F32) + parts[part, rows, :].astype(F32)
                    held[s - 1, rows, :] = total.astype(BF16)
                rs_copy(right, s, sub).start()

    rs_step(0)
    loads[1].wait()
    make_parts(1 - first_half)
    rs_step(1)

    for there in along_x:
        pl.semaphore_signal(near_sem, inc=1, device_id=there, device_id_type=MESH)
    a1 = [Plane(roots_out.at[n], roots_in.at[n], a1_sem.at[n], (z, o)) for n in range(2)]

    def send_roots(n, root):
        loads[2 + n].wait()
        for k in range(4):
            stacked = jnp.concatenate(
                [root[p, 16 * k : 16 * k + 16, 128 * q : 128 * q + 128] for p in range(2) for q in range(8)], axis=0
            )
            roots_out[n, 256 * k : 256 * k + 256, :] = mix(perm[ROOTS_OUT], stacked)
        a1[n].start()

    perm[ROOTS_OUT] = shuffle(roots_out_rows)
    pl.semaphore_wait(near_sem, len(along_x))
    send_roots(0, rroot)
    rs_step(2)
    send_roots(1, lroot)
    rs_step(3)

    loads[4].wait()
    loads[5].wait()
    places = [owner_ref[b] * 2 + slot_ref[b] for b in range(BLOCKS)]
    row, column = iotas(16, WIDTH)
    for b in range(BLOCKS):
        to_blocks[16 * b : 16 * b + 16, :] = one_hot(column == places[b] * 16 + row)
    rs_step(4)

    def make_order(q):
        row, column = iotas(WIDTH, 256)
        chosen = ((column >> 2) & 15) * 64 + 16 * q + ((column >> 6) & 3) * 4 + (column & 3)
        order[:, 256 * q : 256 * q + 256] = one_hot(row == chosen)

    perm[RESULTS_IN] = shuffle(results_in)
    make_order(0)
    make_order(1)
    rs_step(5)

    a1[0].wait(1)
    blocks_out[0] = mix(to_blocks[...], roots_in[0])
    perm[RESULTS_OUT] = shuffle(results_out)
    make_order(2)
    rs_step(6)

    a1[1].wait(1)
    blocks_out[1] = mix(to_blocks[...], roots_in[1])
    make_order(3)
    rs_step(7)

    column = lax.broadcasted_iota(jnp.int32, (1, 512), 1)
    target = jnp.zeros((1, 512), jnp.int32)
    for b in range(BLOCKS):
        target = jnp.where(column // 16 == b, places[b] * 16, target)
    target = target + column % 16
    for k in range(4):
        row = lax.broadcasted_iota(jnp.int32, (256, 512), 0) + 256 * k
        to_places[256 * k : 256 * k + 256, :] = one_hot(row == target)

    def last_sum(which):
        rows = chunk(which * 32, 32)
        for held, sems in ((from_left, right_sem), (from_right, left_sem)):
            for n in range(2):
                ref = held.at[7, chunk(which * 32 + n * 16, 16)]
                pltpu.make_async_copy(ref, ref, sems.at[7, which * 2 + n]).wait()
        total = parts[z, rows, :].astype(F32) + from_left[7, rows, :].astype(F32) + from_right[7, rows, :].astype(F32)
        return total.astype(BF16)

    def swap_copy(rows_of):
        return pltpu.make_async_remote_copy(
            src_ref=swapped,
            dst_ref=block.at[chunk(rows_of * 32, 32)],
            send_sem=swap_sem.at[0],
            recv_sem=swap_sem.at[1],
            device_id=(z, 2 * chip + 1 - c),
            device_id_type=MESH,
        )

    swapped[...] = last_sum(1 - c)
    swap_copy(o).start()
    block[chunk(o * 32, 32), :] = last_sum(c)
    spread = Spread(block, block_send, block_recv, (z, x, y, c))
    spread.begin(0)
    swap_copy(2 * chip + 1 - c).wait_recv()
    spread.begin(1)
    a2 = [Column(blocks_out.at[n], blocks_in.at[n], a2_sem.at[n], (z, chip, c)) for n in range(2)]
    a2[0].start()
    spread.early()
    a2[1].start()
    spread.middle()
    spread.late()

    def rows_of_root(n, held, start):
        a2[n].wait(1)
        for h in range(2):
            turned = mix(perm[RESULTS_IN], blocks_in[n, 256 * h : 256 * h + 256, :])
            for q in range(8):
                held[chunk(start + 32 * h, 32), 128 * q : 128 * q + 128] = turned[32 * q : 32 * q + 32]

    rows_of_root(0, rheld, chip * 64)
    rspread = Spread(rheld, rheld_send, rheld_recv, (z, x, y, c))
    rspread.begin(0)
    rspread.begin(1)
    spread.end()

    def send_rows(n, product):
        for q in range(4):
            rows64[n, :, 256 * q : 256 * q + 256] = product(q).astype(BF16)
        for h in range(2):
            stacked = jnp.concatenate(
                [rows64[n, 32 * h : 32 * h + 32, 128 * q : 128 * q + 128] for q in range(8)], axis=0
            )
            zout[n, 256 * h : 256 * h + 256, :] = mix(perm[RESULTS_OUT], stacked)
        arrive = arrived_ref.at[pl.ds(2048, 512)] if n == 2 else zin.at[n]
        exchange = Column(zout.at[n], arrive, z_sem.at[n], (z, chip, c))
        exchange.start()
        return exchange

    m, k = iotas(64, 256)
    chosen = one_hot(k == (m >> 2) * 16 + 4 * y + (m & 3))
    stacked = jnp.concatenate([block[chunk(64 * zz + 16 * x, 16), :] for zz in range(PLANES)], axis=0)
    lhs = mix(chosen, stacked)
    zl = send_rows(0, lambda q: times_transposed(lhs, block[256 * q : 256 * q + 256, :]))
    m, k = iotas(64, WIDTH)
    chosen = one_hot(k == (m >> 2) * 64 + 4 * chip + (m & 3))
    columns = jnp.concatenate(
        [times_transposed(chosen, block[256 * q : 256 * q + 256, :]).astype(BF16) for q in range(4)], axis=1
    )
    zr = send_rows(1, lambda q: jnp.dot(columns, block[:, 256 * q : 256 * q + 256], preferred_element_type=F32))

    rspread.early()
    rspread.middle()
    rspread.late()
    rows_of_root(1, lsel, 0)
    scaled = jnp.concatenate([mix(lsel[...], block[:, 256 * q : 256 * q + 256]) for q in range(4)], axis=1)
    scaled = jnp.concatenate([mix(scaled, order[:, 256 * q : 256 * q + 256]) for q in range(4)], axis=1)
    rspread.end()
    zp = send_rows(2, lambda q: jnp.dot(scaled, rheld[:, 256 * q : 256 * q + 256], preferred_element_type=F32))

    def to_owners(n, exchange):
        exchange.wait(1)
        stats_out[n] = mix(to_places[...], zin[n])
        owners = Plane(stats_out.at[n], arrived_ref.at[pl.ds(1024 * n, 1024)], f_sem.at[n], (z, o))
        owners.start()
        return owners

    fl = to_owners(0, zl)
    fr = to_owners(1, zr)

    for exchange in (fl, fr, zp):
        exchange.wait(1)

    ref = parts.at[pl.ds(0, 15)]
    pltpu.make_async_copy(ref, ref, rs_send).wait()
    swap_copy(o).wait_send()
    spread.sent()
    rspread.sent()
    for exchange in (*a1, *a2, zl, zr, zp, fl, fr):
        exchange.wait(0)


def finish(arrived_ref, lstat_ref, rstat_ref, precond_ref, left_ref, right_ref):
    turn = shuffle(transpose16)
    for h in range(2):
        turned = mix(turn, arrived_ref[2048 + 256 * h : 2304 + 256 * h, :])
        for n in range(16):
            precond_ref[16 * h : 16 * h + 16, 128 * n : 128 * n + 128] = turned[16 * n : 16 * n + 16]
    turn = shuffle(stats_in)
    for t, (old, new) in enumerate(((lstat_ref, left_ref), (rstat_ref, right_ref))):
        for k in range(4):
            turned = jnp.dot(turn, arrived_ref[1024 * t + 256 * k : 1024 * t + 256 * k + 256, :], preferred_element_type=F32)
            for p in range(2):
                for n in range(8):
                    at = (p * 8 + n) * 16
                    there = (p, slice(16 * k, 16 * k + 16), slice(128 * n, 128 * n + 128))
                    new[there] = decay_rate * old[there] + (1.0 - decay_rate) * turned[at : at + 16]


def step(grad_partials, block_owner, block_slot, left_stat, right_stat, left_root, right_root):
    vmem = pl.BlockSpec(memory_space=pltpu.VMEM)
    hbm = pl.BlockSpec(memory_space=pl.ANY)
    dma = pltpu.SemaphoreType.DMA
    arrived = pl.pallas_call(
        kernel,
        out_shape=jax.ShapeDtypeStruct((2560, 128), BF16),
        in_specs=[hbm] * 5,
        out_specs=vmem,
        scratch_shapes=[
            pltpu.SMEM((BLOCKS,), jnp.int32),
            pltpu.SMEM((BLOCKS,), jnp.int32),
            pltpu.VMEM((32, 32 * WIDTH), BF16),
            pltpu.VMEM((2, 64, WIDTH), BF16),
            pltpu.VMEM((2, 64, WIDTH), BF16),
            pltpu.VMEM((4, 256, 256), BF16),
            pltpu.VMEM((16, 64, WIDTH), BF16),
            pltpu.VMEM((8, 64, WIDTH), BF16),
            pltpu.VMEM((8, 64, WIDTH), BF16),
            pltpu.VMEM((32, WIDTH), BF16),
            pltpu.VMEM((WIDTH, WIDTH), BF16),
            pltpu.VMEM((2, 1024, 128), BF16),
            pltpu.VMEM((2, 1024, 128), BF16),
            pltpu.VMEM((2, 512, 128), BF16),
            pltpu.VMEM((2, 512, 128), BF16),
            pltpu.VMEM((64, WIDTH), BF16),
            pltpu.VMEM((WIDTH, WIDTH), BF16),
            pltpu.VMEM((WIDTH, WIDTH), BF16),
            pltpu.VMEM((3, 64, WIDTH), BF16),
            pltpu.VMEM((3, 512, 128), BF16),
            pltpu.VMEM((2, 512, 128), BF16),
            pltpu.VMEM((2, 1024, 128), BF16),
            pltpu.VMEM((512, 1024), BF16),
            pltpu.VMEM((1024, 512), BF16),
            dma((6,)),
            pltpu.SemaphoreType.REGULAR,
            dma,
            dma((8, SUBS)),
            dma((8, SUBS)),
            dma((2,)),
            dma,
            dma((2, 4, 4, 2)),
            dma,
            dma((2, 4, 4, 2)),
            dma((2, 2)),
            dma((2, 2)),
            dma((3, 2)),
            dma((2, 2)),
        ],
        compiler_params=pltpu.CompilerParams(
            collective_id=0, has_side_effects=True, vmem_limit_bytes=60 * 1024 * 1024
        ),
    )(block_owner, block_slot, grad_partials, left_root, right_root)
    return pl.pallas_call(
        finish,
        out_shape=(
            jax.ShapeDtypeStruct((BLOCKS, 2 * WIDTH), BF16),
            jax.ShapeDtypeStruct(left_stat.shape, F32),
            jax.ShapeDtypeStruct(right_stat.shape, F32),
        ),
        in_specs=[vmem] * 3,
        out_specs=[vmem] * 3,
        compiler_params=pltpu.CompilerParams(vmem_limit_bytes=16 * 1024 * 1024),
    )(arrived, left_stat, right_stat)


def solution(mesh):
    return jax.shard_map(
        step,
        mesh=mesh,
        in_specs=(
            P("dp", None, "owner"),
            P(),
            P(),
            P("owner", "dp", None),
            P("owner", "dp", None),
            P("owner", "dp", None),
            P("owner", "dp", None),
        ),
        out_specs=(P(None, ("dp", "owner")), P("owner", "dp", None), P("owner", "dp", None)),
        check_vma=False,
    )
```
